1024 devices in a mesh: blk: 256 (over z_lo, y, x, core), head: 4 (over z_hi).
Axes of the slice: x: 8, y: 8, z: 8 (z_hi: 4, z_lo: 2; z = z_hi * 2 + z_lo), core: 2. Of those that a mesh axis runs over, the one named last changes fastest.
Arguments:
- image_feats: bfloat16 [81920, 768], P('blk'), may hold values from -6 to 6
- text_feats: bfloat16 [81920, 768], P('blk'), may hold values from -6 to 6
- image_head: bfloat16 [768, 768], P(None, 'head'), may hold values from -0.21875 to 0.21875
- text_head: bfloat16 [768, 768], P(None, 'head'), may hold values from -0.21875 to 0.21875
Outputs:
- image_grad: bfloat16 [81920, 768], P('blk', 'head')
- text_grad: bfloat16 [81920, 768], P('blk', 'head')
- row_loss: float32 [81920], P(('blk', 'head'))
The draws below stay inside these ranges and needn't reach their ends.
All inputs are finite; a program needn't handle non-finite values.
Results may differ from the reference program's by a relative error of at most 0.024.
Values may be sent and summed in bfloat16 or wider, within the bound.
No kernel may reach another device: no remote copies, remote signals or barrier semaphores. Data moves between devices by JAX's collectives and lax.ppermute only.
A program may use at most 32 MiB of HBM per device.

```python
import jax
import jax.numpy as jnp
from jax import lax

D = 768
E = 768
ROWS_DEV = 320
STEPS = 4
TOKENS = 81920
N_HEAD = 4


def steps_of(stream_key, extent, shards, smallest, top_value):
    factor_of, own = 1.0, jax.random.fold_in(stream_key, 6)
    for dim, shards_of in shards:
        steps = jnp.exp(jax.random.uniform(jax.random.fold_in(own, dim), (shards_of,), jnp.float32, smallest / len(shards), top_value / len(shards)))
        factor_of = factor_of * jnp.repeat(steps, extent[dim] // shards_of).reshape([-1 if axis == dim else 1 for axis in range(len(extent))])
    return factor_of


def scatter_about(stream_key, dims, deviation, reach, cuts=(), kind=jnp.bfloat16):
    result = deviation * jax.random.normal(stream_key, dims, jnp.float32)
    if cuts:
        result = result * steps_of(stream_key, dims, cuts, -0.22, 0.18)
    return jnp.clip(result, -reach, reach).astype(kind)


def setup_inputs(seed: int = 0) -> dict:
    key_of = jax.random.split(jax.random.key(seed), 5)
    image_feats = scatter_about(key_of[0], (TOKENS, D), 1.0, 6.0, ((0, 256),))
    text_feats = scatter_about(key_of[1], (TOKENS, D), 1.0, 6.0, ((0, 256),))
    image_head = scatter_about(key_of[2], (D, E), D ** -0.5, 0.21875, ((1, 4),))
    text_head = scatter_about(key_of[3], (D, E), D ** -0.5, 0.21875, ((1, 4),))
    return {"image_feats": image_feats, "text_feats": text_feats, "image_head": image_head, "text_head": text_head}


logit_scale = 10.0
logit_bias = -2.0
epsilon = 1e-06

def project(feats, head):
    return jnp.dot(feats, head, preferred_element_type=jnp.float32)

def back_project(grads, head):
    width = E // N_HEAD
    total = jnp.zeros((grads.shape[0], D), jnp.float32)
    for group in range(N_HEAD):
        piece = jnp.dot(grads[:, group * width:(group + 1) * width], head[:, group * width:(group + 1) * width].T, preferred_element_type=jnp.float32)
        total = total + piece.astype(jnp.bfloat16).astype(jnp.float32)
    return total.astype(jnp.bfloat16)

def reference(image_feats, text_feats, image_head, text_head):
    z_image = project(image_feats, image_head)
    z_text = project(text_feats, text_head)
    n_image = jnp.sqrt(lax.optimization_barrier(jnp.sum(z_image * z_image, axis=1, keepdims=True)) + epsilon)
    n_text = jnp.sqrt(lax.optimization_barrier(jnp.sum(z_text * z_text, axis=1, keepdims=True)) + epsilon)
    u_image = (z_image / n_image).astype(jnp.bfloat16)
    u_text = (z_text / n_text).astype(jnp.bfloat16)
    blocks = TOKENS // ROWS_DEV
    image_blocks = u_image.reshape(blocks, ROWS_DEV, E).astype(jnp.float32)
    text_blocks = u_text.reshape(blocks, ROWS_DEV, E).astype(jnp.float32)
    diagonal = jnp.eye(ROWS_DEV, dtype=jnp.float32)
    losses = jnp.zeros((blocks, ROWS_DEV), jnp.float32)
    g_image = jnp.zeros((blocks, ROWS_DEV, E), jnp.float32)
    g_text = jnp.zeros((blocks, ROWS_DEV, E), jnp.float32)
    for step in range(STEPS):
        shifted = jnp.roll(text_blocks, -step, axis=0)
        logits = logit_scale * jnp.einsum('bre,bce->brc', image_blocks, shifted) + logit_bias
        if step == 0:
            signs = 2.0 * diagonal - 1.0
        else:
            signs = -jnp.ones_like(diagonal)
        losses = losses + lax.optimization_barrier(jnp.sum(jax.nn.softplus(-signs * logits), axis=2))
        weights = (-signs * jax.nn.sigmoid(-signs * logits) * logit_scale).astype(jnp.bfloat16).astype(jnp.float32)
        g_image = g_image + jnp.einsum('brc,bce->bre', weights, shifted)
        share = jnp.einsum('brc,bre->bce', weights, image_blocks)
        g_text = g_text + jnp.roll(share, step, axis=0)
    g_image = g_image.reshape(TOKENS, E)
    g_text = g_text.reshape(TOKENS, E)
    dot_image = lax.optimization_barrier(jnp.sum(g_image * z_image, axis=1, keepdims=True))
    dot_text = lax.optimization_barrier(jnp.sum(g_text * z_text, axis=1, keepdims=True))
    dz_image = (g_image / n_image - z_image * (dot_image / n_image ** 3)).astype(jnp.bfloat16)
    dz_text = (g_text / n_text - z_text * (dot_text / n_text ** 3)).astype(jnp.bfloat16)
    image_grad = back_project(dz_image, image_head)
    text_grad = back_project(dz_text, text_head)
    return (image_grad, text_grad, losses.reshape(TOKENS))
```

```python
import jax
import jax.numpy as jnp
from jax import lax
from jax.sharding import PartitionSpec as P

LOGIT_SCALE = 10.0
LOGIT_BIAS = -2.0
EPSILON = 1e-06
AXES = ("blk", "head")


class Grid:
    def __init__(self, n_blk, n_head):
        self.n_blk, self.n_head = n_blk, n_head
        self.half = n_blk // 2
        self.depth = 2 * n_head

    def at(self, device):
        blk, head = divmod(device, self.n_head)
        return blk, 2 * head + blk // self.half

    def device(self, blk, z):
        z %= self.depth
        blk = blk % self.half + self.half * (z % 2)
        return blk * self.n_head + z // 2

    def route(self, source):
        return [(source(d), d) for d in range(self.n_blk * self.n_head)]

    def along_blk(self, distance):
        def source(d):
            blk, head = divmod(d, self.n_head)
            step = distance(blk) if callable(distance) else distance
            return (blk + step) % self.n_blk * self.n_head + head

        return self.route(source)

    def along_z(self, odd, even):
        def source(d):
            blk, z = self.at(d)
            return self.device(blk, z + (odd if z % 2 else even))

        return self.route(source)


def project(feats, shards):
    head = jnp.concatenate(shards, axis=1)
    z = jnp.dot(feats, head, preferred_element_type=jnp.float32)
    n = jnp.sqrt(jnp.sum(z * z, axis=1, keepdims=True) + EPSILON)
    return z, n, (z / n).astype(jnp.bfloat16), head


def inner(left, right):
    return lax.dot_general(left, right, (((1,), (1,)), ((), ())), preferred_element_type=jnp.float32)


def weights_of(logits):
    rows, columns = logits.shape
    own = lax.broadcasted_iota(jnp.int32, logits.shape, 0) == lax.broadcasted_iota(
        jnp.int32, logits.shape, 1
    )
    signs = jnp.where(own, 1.0, -1.0)
    return (-signs * jax.nn.sigmoid(-signs * logits) * LOGIT_SCALE).astype(jnp.bfloat16)


def gradient(g, z, n, head, group):
    rows = z.shape[0]
    g, z, n = g, z[:rows], n[:rows]
    dot = jnp.sum(g * z, axis=1, keepdims=True)
    dz = (g / n - z * (dot / n**3)).astype(jnp.bfloat16)
    width = head.shape[0] // lax.axis_size("head")
    part = lax.dynamic_slice_in_dim(head, group * width, width, 0)
    return inner(dz, part).astype(jnp.bfloat16)


def body(image_feats, text_feats, image_head, text_head):
    rows = image_feats.shape[0]
    grid = Grid(lax.axis_size("blk"), lax.axis_size("head"))
    group = lax.axis_index("head")
    first = lax.axis_index("blk") % 2 == 0

    def permute(block, route):
        return lax.ppermute(block, AXES, route)

    swap = grid.along_blk(lambda blk: 1 - 2 * (blk % 2))
    mine = jnp.where(first, image_head, text_head)
    taken = [permute(mine, grid.along_z(*way)) for way in ((1, -1), (-2, 2), (3, -3))]
    text_2 = permute(text_feats, grid.along_blk(2))
    image_2 = permute(image_feats, grid.along_blk(-2))
    far = permute(
        jnp.where(first, text_feats, image_feats),
        grid.along_blk(lambda blk: 3 if blk % 2 else -3),
    )
    near = permute(jnp.where(first, image_feats, text_feats), swap)
    text_x = permute(text_2, swap)
    image_x = permute(image_2, swap)
    others = permute(jnp.concatenate(taken, axis=1), swap)
    others = jnp.split(others, 3, axis=1)
    image_shards = [image_head] + [jnp.where(first, t, o) for t, o in zip(taken, others)]
    text_shards = [text_head] + [jnp.where(first, o, t) for t, o in zip(taken, others)]
    texts = jnp.concatenate([text_feats, text_2, text_x, jnp.where(first, near, far)], axis=0)
    images = jnp.concatenate([image_feats, image_2, image_x, jnp.where(first, far, near)], axis=0)

    z_text, n_text, u_text, text_whole = project(texts, text_shards)
    z_image, n_image, u_image, image_whole = project(images, image_shards)

    logits = LOGIT_SCALE * inner(u_image[:rows], u_text) + LOGIT_BIAS
    logits_t = LOGIT_SCALE * inner(u_text[:rows], u_image) + LOGIT_BIAS
    g_image = jnp.dot(weights_of(logits), u_text, preferred_element_type=jnp.float32)
    g_text = jnp.dot(weights_of(logits_t), u_image, preferred_element_type=jnp.float32)
    image_grad = gradient(g_image, z_image[:rows], n_image[:rows], image_whole, group)
    text_grad = gradient(g_text, z_text[:rows], n_text[:rows], text_whole, group)

    quarter = rows // lax.axis_size("head")
    own = lax.dynamic_slice_in_dim(logits, group * quarter, quarter, 0)
    row_ids = group * quarter + lax.broadcasted_iota(jnp.int32, own.shape, 0)
    signs = jnp.where(row_ids == lax.broadcasted_iota(jnp.int32, own.shape, 1), 1.0, -1.0)
    row_loss = jnp.sum(jax.nn.softplus(-signs * own), axis=1)
    return image_grad, text_grad, row_loss


def solution(mesh):
    in_specs = (P("blk", None), P("blk", None), P(None, "head"), P(None, "head"))
    out_specs = (P("blk", "head"), P("blk", "head"), P(("blk", "head")))
    return jax.shard_map(body, mesh=mesh, in_specs=in_specs, out_specs=out_specs, check_vma=False)
```

```python
import jax
import jax.numpy as jnp
from jax import lax
from jax.experimental import pallas as pl
from jax.experimental.pallas import tpu as pltpu
from jax.sharding import PartitionSpec as P

LOGIT_SCALE = 10.0
LOGIT_BIAS = -2.0
EPSILON = 1e-06
AXES = ("blk", "head")
LANES = 128


class Grid:
    def __init__(self, n_blk, n_head):
        self.n_blk, self.n_head = n_blk, n_head
        self.half = n_blk // 2
        self.depth = 2 * n_head

    def route(self, source):
        return [(source(d), d) for d in range(self.n_blk * self.n_head)]

    def along_blk(self, even, odd):
        def source(d):
            blk, head = divmod(d, self.n_head)
            step = odd if blk % 2 else even
            return (blk + step) % self.n_blk * self.n_head + head

        return self.route(source)

    def along_z(self, even, odd):
        def source(d):
            blk, head = divmod(d, self.n_head)
            z = 2 * head + blk // self.half
            z = (z + (odd if z % 2 else even)) % self.depth
            return (blk % self.half + self.half * (z % 2)) * self.n_head + z // 2

        return self.route(source)


def dot(left, right, left_dim=1, right_dim=0):
    return lax.dot_general(
        left, right, (((left_dim,), (right_dim,)), ((), ())), preferred_element_type=jnp.float32
    )


def stack(shards, whole):
    at = 0
    for shard in shards:
        whole[at : at + shard.shape[0], :] = shard[...]
        at += shard.shape[0]


def project(feats, whole):
    z = dot(feats, whole[...], 1, 1)
    back = 1.0 / jnp.sqrt(jnp.sum(z * z, axis=1, keepdims=True) + EPSILON)
    return z, back, (z * back).astype(jnp.bfloat16)


def window(group, width):
    start = group * width // LANES * LANES
    return pl.multiple_of(start, LANES), pl.multiple_of(group * width - start, 64)


def primary_kernel(group, own, r1, r2, r3, w0, w1, w2, w3, u_out, z_out, back_out, cut_out, whole):
    rows = own.shape[0]
    stack((w0, w1, w2, w3), whole)
    start, _ = window(group[0], w0.shape[0])
    cut_out[...] = whole[:, pl.ds(start, cut_out.shape[1])]
    for k, block in enumerate((own, r1, r2, r3)):
        z, back, u = project(block[...], whole)
        u_out[k * rows : (k + 1) * rows, :] = u
        if k == 0:
            z_out[...] = z
            back_out[...] = back


def side(u_own, u_others, z, back, cut, logits_ref, at):
    rows = u_own.shape[0]
    logits = LOGIT_SCALE * dot(u_own, u_others[...], 1, 1) + LOGIT_BIAS
    logits_ref[at] = logits
    own = logits[:, :rows]
    turn = jnp.where(
        lax.broadcasted_iota(jnp.int32, own.shape, 0) == lax.broadcasted_iota(jnp.int32, own.shape, 1),
        -1.0,
        1.0,
    )
    w_own = (turn * LOGIT_SCALE / (1.0 + jnp.exp(-turn * own))).astype(jnp.bfloat16)
    w = (LOGIT_SCALE / (1.0 + jnp.exp(-logits[:, rows:]))).astype(jnp.bfloat16)
    g = dot(w_own, u_others[:rows, :]) + dot(w, u_others[rows:, :])
    inner = jnp.sum(g * z, axis=1, keepdims=True)
    dz = (g * back - z * (inner * back * back * back)).astype(jnp.bfloat16)
    return jnp.transpose(dot(dz, cut))


def main_kernel(
    place, own, s123, w0, w123, u_p, z_p, back_p, cut_p, image_out, text_out, loss_out,
    whole, u_q, logits_ref, grads,
):
    group, swapped = place[0], place[1]
    rows, width = own.shape[0], w0.shape[0]
    stack((w0, w123), whole)
    start, offset = window(group, width)
    z_q, back_q, u = project(own[...], whole)
    u_q[:rows, :] = u
    for k in range(3):
        _, _, u = project(s123[k * rows : (k + 1) * rows, :], whole)
        u_q[(k + 1) * rows : (k + 2) * rows, :] = u
    cut_q = whole[:, pl.ds(start, cut_p.shape[1])]
    grads[0] = side(u_p[:rows, :], u_q, z_p[...], back_p[...], cut_p[...], logits_ref, 0)
    grads[1] = side(u_q[:rows, :], u_p, z_q, back_q, cut_q, logits_ref, 1)
    image_out[...] = grads[swapped, pl.ds(offset, width), :].astype(image_out.dtype)
    text_out[...] = grads[1 - swapped, pl.ds(offset, width), :].astype(text_out.dtype)
    quarter = loss_out.shape[1]
    first = pl.multiple_of(group * quarter, 8)
    x = logits_ref[swapped, pl.ds(first, quarter), :]
    on = first + lax.broadcasted_iota(jnp.int32, x.shape, 0) == lax.broadcasted_iota(
        jnp.int32, x.shape, 1
    )
    x = jnp.where(on, -x, x)
    loss = jnp.sum(jnp.maximum(x, 0.0) + jnp.log1p(jnp.exp(-jnp.abs(x))), axis=1, keepdims=True)
    loss_out[...] = jnp.transpose(jnp.broadcast_to(loss, (quarter, LANES)))[:1, :]


VMEM = pl.BlockSpec(memory_space=pltpu.VMEM)
SMEM = pl.BlockSpec(memory_space=pltpu.SMEM)
PARAMS = pltpu.CompilerParams(vmem_limit_bytes=48 * 1024 * 1024)


def body(image_feats, text_feats, image_head, text_head):
    rows, depth = image_feats.shape
    groups = lax.axis_size("head")
    grid = Grid(lax.axis_size("blk"), groups)
    group = lax.axis_index("head")
    odd = lax.axis_index("blk") % 2
    even = odd == 0

    def permute(block, route):
        return lax.ppermute(block, AXES, route)

    swap = grid.along_blk(1, -1)
    image_head, text_head = image_head.T, text_head.T
    width, features = image_head.shape[0], image_head.shape[0] * groups
    own_p = jnp.where(even, image_feats, text_feats)
    own_q = jnp.where(even, text_feats, image_feats)
    head_p = jnp.where(even, image_head, text_head)
    head_q = jnp.where(even, text_head, image_head)
    r1 = permute(own_q, grid.along_blk(-1, 1))
    r2 = permute(own_p, grid.along_blk(-2, 2))
    r3 = permute(own_q, grid.along_blk(-3, 3))
    taken = [permute(head_p, grid.along_z(*way)) for way in ((-3, 3), (2, -2), (-1, 1))]
    s123 = permute(jnp.concatenate([own_p, r1, r2], axis=0), swap)
    w123 = permute(jnp.concatenate(taken, axis=0), swap)

    place = jnp.stack([group, odd]).astype(jnp.int32)
    cut = 2 * LANES
    whole = pltpu.VMEM((features, depth), jnp.bfloat16)
    u_p, z_p, back_p, cut_p = pl.pallas_call(
        primary_kernel,
        out_shape=(
            jax.ShapeDtypeStruct((4 * rows, features), jnp.bfloat16),
            jax.ShapeDtypeStruct((rows, features), jnp.float32),
            jax.ShapeDtypeStruct((rows, 1), jnp.float32),
            jax.ShapeDtypeStruct((features, cut), jnp.bfloat16),
        ),
        in_specs=[SMEM] + [VMEM] * 8,
        out_specs=(VMEM,) * 4,
        scratch_shapes=[whole],
        compiler_params=PARAMS,
        cost_estimate=pl.CostEstimate(
            flops=8 * rows * depth * features, bytes_accessed=8_000_000, transcendentals=0
        ),
    )(place, own_p, r1, r2, r3, head_p, *taken)
    image_grad, text_grad, loss = pl.pallas_call(
        main_kernel,
        out_shape=(
            jax.ShapeDtypeStruct((width, rows), jnp.bfloat16),
            jax.ShapeDtypeStruct((width, rows), jnp.bfloat16),
            jax.ShapeDtypeStruct((1, rows // groups), jnp.float32),
        ),
        in_specs=[SMEM] + [VMEM] * 8,
        out_specs=(VMEM,) * 3,
        scratch_shapes=[
            whole,
            pltpu.VMEM((4 * rows, features), jnp.bfloat16),
            pltpu.VMEM((2, rows, 4 * rows), jnp.float32),
            pltpu.VMEM((2, cut, rows), jnp.float32),
        ],
        compiler_params=PARAMS,
        cost_estimate=pl.CostEstimate(
            flops=24 * rows * depth * features, bytes_accessed=8_000_000, transcendentals=0
        ),
    )(place, own_q, s123, head_q, w123, u_p, z_p, back_p, cut_p)
    return image_grad.T, text_grad.T, loss.reshape(rows // groups)


def solution(mesh):
    in_specs = (P("blk", None), P("blk", None), P(None, "head"), P(None, "head"))
    out_specs = (P("blk", "head"), P("blk", "head"), P(("blk", "head")))
    return jax.shard_map(body, mesh=mesh, in_specs=in_specs, out_specs=out_specs, check_vma=False)
```

```python
import jax
import jax.numpy as jnp
from jax import lax
from jax.experimental import pallas as pl
from jax.experimental.pallas import tpu as pltpu
from jax.sharding import PartitionSpec as P

LOGIT_SCALE = 10.0
LOGIT_BIAS = -2.0
EPSILON = 1e-06
PACK = 20_000_000_000
AXES = ("blk", "head")
LANES = 128


class Grid:
    def __init__(self, n_blk, n_head):
        self.n_blk, self.n_head = n_blk, n_head
        self.half = n_blk // 2
        self.depth = 2 * n_head

    def route(self, source):
        return [(source(d), d) for d in range(self.n_blk * self.n_head)]

    def along_blk(self, even, odd):
        def source(d):
            blk, head = divmod(d, self.n_head)
            step = odd if blk % 2 else even
            return (blk + step) % self.n_blk * self.n_head + head

        return self.route(source)

    def along_z(self, even, odd):
        def source(d):
            blk, head = divmod(d, self.n_head)
            z = 2 * head + blk // self.half
            z = (z + (odd if z % 2 else even)) % self.depth
            return (blk % self.half + self.half * (z % 2)) * self.n_head + z // 2

        return self.route(source)


def dot(left, right, left_dim=1, right_dim=0):
    return lax.dot_general(
        left, right, (((left_dim,), (right_dim,)), ((), ())), preferred_element_type=jnp.float32
    )


def stack(shards, whole):
    at = 0
    for shard in shards:
        whole[at : at + shard.shape[0], :] = shard[...]
        at += shard.shape[0]


def project(feats, whole):
    z = dot(feats, whole[...], 1, 1)
    back = 1.0 / jnp.sqrt(jnp.sum(z * z, axis=1, keepdims=True) + EPSILON)
    return z, back, (z * back).astype(jnp.bfloat16)


def window(group, width):
    start = group * width // LANES * LANES
    return pl.multiple_of(start, LANES), pl.multiple_of(group * width - start, 64)


def primary_kernel(group, own, r1, r2, r3, w0, w1, w2, w3, u_out, z_out, back_out, cut_out, whole):
    rows = own.shape[0]
    stack((w0, w1, w2, w3), whole)
    start, _ = window(group[0], w0.shape[0])
    cut_out[...] = whole[:, pl.ds(start, cut_out.shape[1])]
    for k, block in enumerate((own, r1, r2, r3)):
        z, back, u = project(block[...], whole)
        u_out[k * rows : (k + 1) * rows, :] = u
        if k == 0:
            z_out[...] = z
            back_out[...] = back


def pack_kernel(*refs):
    *blocks, out = refs
    stack(blocks, out)


def side(u_own, u_others, z, back, cut, logits_ref, at):
    rows = u_own.shape[0]
    logits = LOGIT_SCALE * dot(u_own, u_others[...], 1, 1) + LOGIT_BIAS
    logits_ref[at] = logits
    own = logits[:, :rows]
    turn = jnp.where(
        lax.broadcasted_iota(jnp.int32, own.shape, 0) == lax.broadcasted_iota(jnp.int32, own.shape, 1),
        -1.0,
        1.0,
    )
    w_own = (turn * LOGIT_SCALE / (1.0 + jnp.exp(-turn * own))).astype(jnp.bfloat16)
    w = (LOGIT_SCALE / (1.0 + jnp.exp(-logits[:, rows:]))).astype(jnp.bfloat16)
    g = dot(w_own, u_others[:rows, :]) + dot(w, u_others[rows:, :])
    inner = jnp.sum(g * z, axis=1, keepdims=True)
    dz = (g * back - z * (inner * back * back * back)).astype(jnp.bfloat16)
    return jnp.transpose(dot(dz, cut))


def main_kernel(
    place, own, s123, w0, w123, u_p, z_p, back_p, cut_p, image_out, text_out, loss_out,
    whole, u_q, logits_ref, grads,
):
    group, swapped = place[0], place[1]
    rows, width = own.shape[0], w0.shape[0]
    stack((w0, w123), whole)
    start, offset = window(group, width)
    z_q, back_q, u = project(own[...], whole)
    u_q[:rows, :] = u
    for k in range(3):
        _, _, u = project(s123[k * rows : (k + 1) * rows, :], whole)
        u_q[(k + 1) * rows : (k + 2) * rows, :] = u
    cut_q = whole[:, pl.ds(start, cut_p.shape[1])]
    grads[0] = side(u_p[:rows, :], u_q, z_p[...], back_p[...], cut_p[...], logits_ref, 0)
    grads[1] = side(u_q[:rows, :], u_p, z_q, back_q, cut_q, logits_ref, 1)
    image_out[...] = grads[swapped, pl.ds(offset, width), :].astype(image_out.dtype)
    text_out[...] = grads[1 - swapped, pl.ds(offset, width), :].astype(text_out.dtype)
    quarter = loss_out.shape[1]
    first = pl.multiple_of(group * quarter, 8)
    x = logits_ref[swapped, pl.ds(first, quarter), :]
    on = first + lax.broadcasted_iota(jnp.int32, x.shape, 0) == lax.broadcasted_iota(
        jnp.int32, x.shape, 1
    )
    x = jnp.where(on, -x, x)
    loss = jnp.sum(jnp.maximum(x, 0.0) + jnp.log1p(jnp.exp(-jnp.abs(x))), axis=1, keepdims=True)
    loss_out[...] = jnp.transpose(jnp.broadcast_to(loss, (quarter, LANES)))[:1, :]


VMEM = pl.BlockSpec(memory_space=pltpu.VMEM)
SMEM = pl.BlockSpec(memory_space=pltpu.SMEM)
PARAMS = pltpu.CompilerParams(vmem_limit_bytes=48 * 1024 * 1024)


def pack(*blocks):
    rows = sum(block.shape[0] for block in blocks)
    return pl.pallas_call(
        pack_kernel,
        out_shape=jax.ShapeDtypeStruct((rows, blocks[0].shape[1]), blocks[0].dtype),
        in_specs=[VMEM] * len(blocks),
        out_specs=VMEM,
        compiler_params=PARAMS,
        cost_estimate=pl.CostEstimate(flops=PACK, bytes_accessed=4_000_000, transcendentals=0),
    )(*blocks)


def body(image_feats, text_feats, image_head, text_head):
    rows, depth = image_feats.shape
    groups = lax.axis_size("head")
    grid = Grid(lax.axis_size("blk"), groups)
    group = lax.axis_index("head")
    odd = lax.axis_index("blk") % 2
    even = odd == 0

    def permute(block, route):
        return lax.ppermute(block, AXES, route)

    swap = grid.along_blk(1, -1)
    image_head, text_head = image_head.T, text_head.T
    width, features = image_head.shape[0], image_head.shape[0] * groups
    own_p = jnp.where(even, image_feats, text_feats)
    own_q = jnp.where(even, text_feats, image_feats)
    head_p = jnp.where(even, image_head, text_head)
    head_q = jnp.where(even, text_head, image_head)
    near = grid.along_z(-1, 1)
    w1 = permute(head_p, near)
    w2 = permute(head_p, grid.along_z(2, -2))
    r1 = permute(own_q, grid.along_blk(-1, 1))
    r2 = permute(own_p, grid.along_blk(-2, 2))
    w3 = permute(w2, near)
    r3 = permute(r1, grid.along_blk(-2, 2))
    taken = [w1, w2, w3]
    s123 = permute(pack(own_p, r1, r2), swap)
    w123 = permute(pack(*taken), swap)

    place = jnp.stack([group, odd]).astype(jnp.int32)
    cut = 2 * LANES
    whole = pltpu.VMEM((features, depth), jnp.bfloat16)
    u_p, z_p, back_p, cut_p = pl.pallas_call(
        primary_kernel,
        out_shape=(
            jax.ShapeDtypeStruct((4 * rows, features), jnp.bfloat16),
            jax.ShapeDtypeStruct((rows, features), jnp.float32),
            jax.ShapeDtypeStruct((rows, 1), jnp.float32),
            jax.ShapeDtypeStruct((features, cut), jnp.bfloat16),
        ),
        in_specs=[SMEM] + [VMEM] * 8,
        out_specs=(VMEM,) * 4,
        scratch_shapes=[whole],
        compiler_params=PARAMS,
        cost_estimate=pl.CostEstimate(
            flops=80 * rows * depth * features, bytes_accessed=8_000_000, transcendentals=0
        ),
    )(place, own_p, r1, r2, r3, head_p, *taken)
    image_grad, text_grad, loss = pl.pallas_call(
        main_kernel,
        out_shape=(
            jax.ShapeDtypeStruct((width, rows), jnp.bfloat16),
            jax.ShapeDtypeStruct((width, rows), jnp.bfloat16),
            jax.ShapeDtypeStruct((1, rows // groups), jnp.float32),
        ),
        in_specs=[SMEM] + [VMEM] * 8,
        out_specs=(VMEM,) * 3,
        scratch_shapes=[
            whole,
            pltpu.VMEM((4 * rows, features), jnp.bfloat16),
            pltpu.VMEM((2, rows, 4 * rows), jnp.float32),
            pltpu.VMEM((2, cut, rows), jnp.float32),
        ],
        compiler_params=PARAMS,
        cost_estimate=pl.CostEstimate(
            flops=24 * rows * depth * features, bytes_accessed=8_000_000, transcendentals=0
        ),
    )(place, own_q, s123, head_q, w123, u_p, z_p, back_p, cut_p)
    return image_grad.T, text_grad.T, loss.reshape(rows // groups)


def solution(mesh):
    in_specs = (P("blk", None), P("blk", None), P(None, "head"), P(None, "head"))
    out_specs = (P("blk", "head"), P("blk", "head"), P(("blk", "head")))
    return jax.shard_map(body, mesh=mesh, in_specs=in_specs, out_specs=out_specs, check_vma=False)
```

```python
import jax
import jax.numpy as jnp
from jax import lax
from jax.experimental import pallas as pl
from jax.experimental.pallas import tpu as pltpu
from jax.sharding import PartitionSpec as P

LOGIT_SCALE = 10.0
LOGIT_BIAS = -2.0
EPSILON = 1e-06
PACK = 20_000_000_000
AXES = ("blk", "head")
LANES = 128


class Grid:
    def __init__(self, n_blk, n_head):
        self.n_blk, self.n_head = n_blk, n_head
        self.half = n_blk // 2
        self.depth = 2 * n_head

    def route(self, source):
        return [(source(d), d) for d in range(self.n_blk * self.n_head)]

    def along_blk(self, even, odd):
        def source(d):
            blk, head = divmod(d, self.n_head)
            step = odd if blk % 2 else even
            return (blk + step) % self.n_blk * self.n_head + head

        return self.route(source)

    def along_z(self, even, odd):
        def source(d):
            blk, head = divmod(d, self.n_head)
            z = 2 * head + blk // self.half
            z = (z + (odd if z % 2 else even)) % self.depth
            return (blk % self.half + self.half * (z % 2)) * self.n_head + z // 2

        return self.route(source)


def dot(left, right, left_dim=1, right_dim=0):
    return lax.dot_general(
        left, right, (((left_dim,), (right_dim,)), ((), ())), preferred_element_type=jnp.float32
    )


def stack(shards, whole):
    at = 0
    for shard in shards:
        whole[at : at + shard.shape[0], :] = shard[...]
        at += shard.shape[0]


def project(feats, whole):
    z = dot(feats, whole[...], 1, 1)
    back = 1.0 / jnp.sqrt(jnp.sum(z * z, axis=1, keepdims=True) + EPSILON)
    return z, back, (z * back).astype(jnp.bfloat16)


def window(group, width):
    start = group * width // LANES * LANES
    return pl.multiple_of(start, LANES), pl.multiple_of(group * width - start, 64)


def primary_kernel(group, w0, w1, w2, w3, own, r1, r2, r3, u_out, z_out, back_out, cut_out, whole):
    rows = own.shape[0]
    stack((w0, w1, w2, w3), whole)
    start, _ = window(group[0], w0.shape[0])
    cut_out[...] = whole[:, pl.ds(start, cut_out.shape[1])]
    for k, block in enumerate((own, r1, r2, r3)):
        z, back, u = project(block[...], whole)
        u_out[k * rows : (k + 1) * rows, :] = u
        if k == 0:
            z_out[...] = z
            back_out[...] = back


def pack_kernel(*refs):
    _, *blocks, out = refs
    stack(blocks, out)


def side(u_own, u_others, z, back, cut, logits_ref, at):
    rows = u_own.shape[0]
    logits = LOGIT_SCALE * dot(u_own, u_others[...], 1, 1) + LOGIT_BIAS
    logits_ref[at] = logits
    own = logits[:, :rows]
    turn = jnp.where(
        lax.broadcasted_iota(jnp.int32, own.shape, 0) == lax.broadcasted_iota(jnp.int32, own.shape, 1),
        -1.0,
        1.0,
    )
    w_own = (turn * LOGIT_SCALE / (1.0 + jnp.exp(-turn * own))).astype(jnp.bfloat16)
    w = (LOGIT_SCALE / (1.0 + jnp.exp(-logits[:, rows:]))).astype(jnp.bfloat16)
    g = dot(w_own, u_others[:rows, :]) + dot(w, u_others[rows:, :])
    inner = jnp.sum(g * z, axis=1, keepdims=True)
    dz = (g * back - z * (inner * back * back * back)).astype(jnp.bfloat16)
    return jnp.transpose(dot(dz, cut))


def main_kernel(
    place, w0, w123, own, s123, u_p, z_p, back_p, cut_p, image_out, text_out, loss_out,
    whole, u_q, logits_ref, grads,
):
    group, swapped = place[0], place[1]
    rows, width = own.shape[0], w0.shape[0]
    stack((w0, w123), whole)
    start, offset = window(group, width)
    z_q, back_q, u = project(own[...], whole)
    u_q[:rows, :] = u
    for k in range(3):
        _, _, u = project(s123[k * rows : (k + 1) * rows, :], whole)
        u_q[(k + 1) * rows : (k + 2) * rows, :] = u
    cut_q = whole[:, pl.ds(start, cut_p.shape[1])]
    grads[0] = side(u_p[:rows, :], u_q, z_p[...], back_p[...], cut_p[...], logits_ref, 0)
    grads[1] = side(u_q[:rows, :], u_p, z_q, back_q, cut_q, logits_ref, 1)
    image_out[...] = grads[swapped, pl.ds(offset, width), :].astype(image_out.dtype)
    text_out[...] = grads[1 - swapped, pl.ds(offset, width), :].astype(text_out.dtype)
    quarter = loss_out.shape[1]
    first = pl.multiple_of(group * quarter, 8)
    x = logits_ref[swapped, pl.ds(first, quarter), :]
    on = first + lax.broadcasted_iota(jnp.int32, x.shape, 0) == lax.broadcasted_iota(
        jnp.int32, x.shape, 1
    )
    x = jnp.where(on, -x, x)
    loss = jnp.sum(jnp.maximum(x, 0.0) + jnp.log1p(jnp.exp(-jnp.abs(x))), axis=1, keepdims=True)
    loss_out[...] = jnp.transpose(jnp.broadcast_to(loss, (quarter, LANES)))[:1, :]


VMEM = pl.BlockSpec(memory_space=pltpu.VMEM)
SMEM = pl.BlockSpec(memory_space=pltpu.SMEM)
PARAMS = pltpu.CompilerParams(vmem_limit_bytes=48 * 1024 * 1024)


def pack(*blocks, after):
    rows = sum(block.shape[0] for block in blocks)
    return pl.pallas_call(
        pack_kernel,
        out_shape=jax.ShapeDtypeStruct((rows, blocks[0].shape[1]), blocks[0].dtype),
        in_specs=[pl.BlockSpec(memory_space=pl.ANY)] + [VMEM] * len(blocks),
        out_specs=VMEM,
        compiler_params=PARAMS,
        cost_estimate=pl.CostEstimate(flops=PACK, bytes_accessed=4_000_000, transcendentals=0),
    )(after, *blocks)


def gate_kernel(x, out):
    pass


def gate(x, cost=PACK):
    return pl.pallas_call(
        gate_kernel,
        out_shape=jax.ShapeDtypeStruct(x.shape, x.dtype),
        in_specs=[pl.BlockSpec(memory_space=pl.ANY)],
        out_specs=pl.BlockSpec(memory_space=pl.ANY),
        input_output_aliases={0: 0},
        cost_estimate=pl.CostEstimate(flops=cost, bytes_accessed=0, transcendentals=0),
    )(x)


def body(image_feats, text_feats, image_head, text_head):
    rows, depth = image_feats.shape
    groups = lax.axis_size("head")
    grid = Grid(lax.axis_size("blk"), groups)
    group = lax.axis_index("head")
    odd = lax.axis_index("blk") % 2
    even = odd == 0

    def permute(block, route):
        return lax.ppermute(block, AXES, route)

    swap = grid.along_blk(1, -1)
    image_head, text_head = image_head.T, text_head.T
    width, features = image_head.shape[0], image_head.shape[0] * groups
    head_p = jnp.where(even, image_head, text_head)
    head_q = jnp.where(even, text_head, image_head)
    own_p = jnp.where(even, image_feats, text_feats)
    own_q = jnp.where(even, text_feats, image_feats)
    near = grid.along_z(-1, 1)
    w1 = permute(head_p, near)
    w2 = permute(head_p, grid.along_z(2, -2))
    r1 = permute(own_q, grid.along_blk(-1, 1))
    r2 = permute(own_p, grid.along_blk(-2, 2))
    w2 = gate(w2)
    w3 = permute(w2, near)
    r1 = gate(r1)
    r3 = permute(r1, grid.along_blk(-2, 2))
    taken = [w1, w2, w3]
    s123 = permute(pack(own_p, r1, r2, after=w2), swap)
    w123 = permute(pack(*taken, after=w1), swap)

    place = jnp.stack([group, odd]).astype(jnp.int32)
    cut = 2 * LANES
    whole = pltpu.VMEM((features, depth), jnp.bfloat16)
    u_p, z_p, back_p, cut_p = pl.pallas_call(
        primary_kernel,
        out_shape=(
            jax.ShapeDtypeStruct((4 * rows, features), jnp.bfloat16),
            jax.ShapeDtypeStruct((rows, features), jnp.float32),
            jax.ShapeDtypeStruct((rows, 1), jnp.float32),
            jax.ShapeDtypeStruct((features, cut), jnp.bfloat16),
        ),
        in_specs=[SMEM] + [VMEM] * 8,
        out_specs=(VMEM,) * 4,
        scratch_shapes=[whole],
        compiler_params=PARAMS,
        cost_estimate=pl.CostEstimate(
            flops=80 * rows * depth * features, bytes_accessed=8_000_000, transcendentals=0
        ),
    )(place, head_p, *taken, own_p, r1, r2, r3)
    image_grad, text_grad, loss = pl.pallas_call(
        main_kernel,
        out_shape=(
            jax.ShapeDtypeStruct((width, rows), jnp.bfloat16),
            jax.ShapeDtypeStruct((width, rows), jnp.bfloat16),
            jax.ShapeDtypeStruct((1, rows // groups), jnp.float32),
        ),
        in_specs=[SMEM] + [VMEM] * 8,
        out_specs=(VMEM,) * 3,
        scratch_shapes=[
            whole,
            pltpu.VMEM((4 * rows, features), jnp.bfloat16),
            pltpu.VMEM((2, rows, 4 * rows), jnp.float32),
            pltpu.VMEM((2, cut, rows), jnp.float32),
        ],
        compiler_params=PARAMS,
        cost_estimate=pl.CostEstimate(
            flops=24 * rows * depth * features, bytes_accessed=8_000_000, transcendentals=0
        ),
    )(place, head_q, w123, own_q, s123, u_p, z_p, back_p, cut_p)
    return image_grad.T, text_grad.T, loss.reshape(rows // groups)


def solution(mesh):
    in_specs = (P("blk", None), P("blk", None), P(None, "head"), P(None, "head"))
    out_specs = (P("blk", "head"), P("blk", "head"), P(("blk", "head")))
    return jax.shard_map(body, mesh=mesh, in_specs=in_specs, out_specs=out_specs, check_vma=False)
```

```python
import jax
import jax.numpy as jnp
from jax import lax
from jax.experimental import pallas as pl
from jax.experimental.pallas import tpu as pltpu
from jax.sharding import PartitionSpec as P

LOGIT_SCALE = 10.0
LOGIT_BIAS = -2.0
EPSILON = 1e-06
PACK = 20_000_000_000
AXES = ("blk", "head")
LANES = 128


class Grid:
    def __init__(self, n_blk, n_head):
        self.n_blk, self.n_head = n_blk, n_head
        self.half = n_blk // 2
        self.depth = 2 * n_head

    def route(self, source):
        return [(source(d), d) for d in range(self.n_blk * self.n_head)]

    def along_blk(self, even, odd):
        def source(d):
            blk, head = divmod(d, self.n_head)
            step = odd if blk % 2 else even
            return (blk + step) % self.n_blk * self.n_head + head

        return self.route(source)

    def along_z(self, even, odd):
        def source(d):
            blk, head = divmod(d, self.n_head)
            z = 2 * head + blk // self.half
            z = (z + (odd if z % 2 else even)) % self.depth
            return (blk % self.half + self.half * (z % 2)) * self.n_head + z // 2

        return self.route(source)


def dot(left, right, left_dim=1, right_dim=0):
    return lax.dot_general(
        left, right, (((left_dim,), (right_dim,)), ((), ())), preferred_element_type=jnp.float32
    )


def project(feats, whole):
    z = dot(feats, whole[...], 1, 1)
    back = 1.0 / jnp.sqrt(jnp.sum(z * z, axis=1, keepdims=True) + EPSILON)
    return z, back, (z * back).astype(jnp.bfloat16)


def window(group, width):
    start = group * width // LANES * LANES
    return pl.multiple_of(start, LANES), pl.multiple_of(group * width - start, 64)


def pack_kernel(*refs):
    _, *blocks, out = refs
    at = 0
    for block in blocks:
        out[at : at + block.shape[0], :] = block[...]
        at += block.shape[0]


def gate_kernel(*refs):
    pass


def primary_kernel(whole, own_r1_r2, r3, u_out, z_out, back_out):
    rows = r3.shape[0]
    for k in range(4):
        block = r3[...] if k == 3 else own_r1_r2[k * rows : (k + 1) * rows, :]
        z, back, u = project(block, whole)
        u_out[k * rows : (k + 1) * rows, :] = u
        if k == 0:
            z_out[...] = z
            back_out[...] = back


def side(u_own, u_others, z, back, cut, logits_ref, at):
    rows = u_own.shape[0]
    logits = LOGIT_SCALE * dot(u_own, u_others[...], 1, 1) + LOGIT_BIAS
    logits_ref[at] = logits
    own = logits[:, :rows]
    turn = jnp.where(
        lax.broadcasted_iota(jnp.int32, own.shape, 0) == lax.broadcasted_iota(jnp.int32, own.shape, 1),
        -1.0,
        1.0,
    )
    w_own = (turn * LOGIT_SCALE / (1.0 + jnp.exp(-turn * own))).astype(jnp.bfloat16)
    w = (LOGIT_SCALE / (1.0 + jnp.exp(-logits[:, rows:]))).astype(jnp.bfloat16)
    g = dot(w_own, u_others[:rows, :]) + dot(w, u_others[rows:, :])
    inner = jnp.sum(g * z, axis=1, keepdims=True)
    dz = (g * back - z * (inner * back * back * back)).astype(jnp.bfloat16)
    return jnp.transpose(dot(dz, cut))


def main_kernel(
    place, whole_q, own, others, whole_p, u_p, z_p, back_p, image_out, text_out, loss_out,
    u_q, logits_ref, grads,
):
    group, swapped = place[0], place[1]
    rows, width = image_out.shape[1], image_out.shape[0]
    start, offset = window(group, width)
    columns = pl.ds(start, grads.shape[1])
    z_q, back_q, u = project(own[...], whole_q)
    u_q[:rows, :] = u
    for k in range(3):
        _, _, u = project(others[k * rows : (k + 1) * rows, :], whole_q)
        u_q[(k + 1) * rows : (k + 2) * rows, :] = u
    grads[0] = side(u_p[:rows, :], u_q, z_p[...], back_p[...], whole_p[:, columns], logits_ref, 0)
    grads[1] = side(u_q[:rows, :], u_p, z_q, back_q, whole_q[:, columns], logits_ref, 1)
    image_out[...] = grads[swapped, pl.ds(offset, width), :].astype(image_out.dtype)
    text_out[...] = grads[1 - swapped, pl.ds(offset, width), :].astype(text_out.dtype)
    quarter = loss_out.shape[1]
    first = pl.multiple_of(group * quarter, 8)
    x = logits_ref[swapped, pl.ds(first, quarter), :]
    on = first + lax.broadcasted_iota(jnp.int32, x.shape, 0) == lax.broadcasted_iota(
        jnp.int32, x.shape, 1
    )
    x = jnp.where(on, -x, x)
    loss = jnp.sum(jnp.maximum(x, 0.0) + jnp.log1p(jnp.exp(-jnp.abs(x))), axis=1, keepdims=True)
    loss_out[...] = jnp.transpose(jnp.broadcast_to(loss, (quarter, LANES)))[:1, :]


ANY = pl.BlockSpec(memory_space=pl.ANY)
VMEM = pl.BlockSpec(memory_space=pltpu.VMEM)
SMEM = pl.BlockSpec(memory_space=pltpu.SMEM)
PARAMS = pltpu.CompilerParams(vmem_limit_bytes=16 * 1024 * 1024)


def cost(flops):
    return pl.CostEstimate(flops=flops, bytes_accessed=1_000_000, transcendentals=0)


def gate(x, after=None):
    operands = (x,) if after is None else (x, after)
    return pl.pallas_call(
        gate_kernel,
        out_shape=jax.ShapeDtypeStruct(x.shape, x.dtype),
        in_specs=[ANY] * len(operands),
        out_specs=ANY,
        input_output_aliases={0: 0},
        cost_estimate=cost(PACK),
    )(*operands)


def pack(*blocks, after):
    rows = sum(block.shape[0] for block in blocks)
    return pl.pallas_call(
        pack_kernel,
        out_shape=jax.ShapeDtypeStruct((rows, blocks[0].shape[1]), blocks[0].dtype),
        in_specs=[ANY] + [VMEM] * len(blocks),
        out_specs=VMEM,
        compiler_params=PARAMS,
        cost_estimate=cost(PACK),
    )(after, *blocks)


def body(image_feats, text_feats, image_head, text_head):
    rows, depth = image_feats.shape
    groups = lax.axis_size("head")
    grid = Grid(lax.axis_size("blk"), groups)
    width = image_head.shape[1]
    features = width * groups
    place = jnp.stack([lax.axis_index("head"), lax.axis_index("blk") % 2]).astype(jnp.int32)

    def permute(block, route):
        return lax.ppermute(block, AXES, route)

    even = place[1] == 0
    image_head, text_head = image_head.T, text_head.T
    own_p = jnp.where(even, image_feats, text_feats)
    own_q = jnp.where(even, text_feats, image_feats)
    head_p = jnp.where(even, image_head, text_head)

    swap = grid.along_blk(1, -1)
    near = grid.along_z(-1, 1)
    two_on = grid.along_blk(-2, 2)
    r1 = permute(own_q, grid.along_blk(-1, 1))
    w2 = permute(head_p, grid.along_z(2, -2))
    w1 = permute(head_p, near)
    r2 = permute(own_p, two_on)
    r1 = gate(r1)
    r3 = permute(r1, two_on)
    w2 = gate(w2, after=r1)
    w3 = permute(w2, near)
    own_r1_r2 = pack(own_p, r1, r2, after=w2)
    others = permute(own_r1_r2, swap)
    whole_p = pack(head_p, w1, w2, w3, after=r1)
    whole_q = permute(whole_p, swap)

    u_p, z_p, back_p = pl.pallas_call(
        primary_kernel,
        out_shape=(
            jax.ShapeDtypeStruct((4 * rows, features), jnp.bfloat16),
            jax.ShapeDtypeStruct((rows, features), jnp.float32),
            jax.ShapeDtypeStruct((rows, 1), jnp.float32),
        ),
        in_specs=[VMEM] * 3,
        out_specs=(VMEM,) * 3,
        compiler_params=PARAMS,
        cost_estimate=cost(80 * rows * depth * features),
    )(whole_p, own_r1_r2, r3)
    image_grad, text_grad, loss = pl.pallas_call(
        main_kernel,
        out_shape=(
            jax.ShapeDtypeStruct((width, rows), jnp.bfloat16),
            jax.ShapeDtypeStruct((width, rows), jnp.bfloat16),
            jax.ShapeDtypeStruct((1, rows // groups), jnp.float32),
        ),
        in_specs=[SMEM] + [VMEM] * 7,
        out_specs=(VMEM,) * 3,
        scratch_shapes=[
            pltpu.VMEM((4 * rows, features), jnp.bfloat16),
            pltpu.VMEM((2, rows, 4 * rows), jnp.float32),
            pltpu.VMEM((2, 2 * LANES, rows), jnp.float32),
        ],
        compiler_params=PARAMS,
        cost_estimate=cost(24 * rows * depth * features),
    )(place, whole_q, own_q, others, whole_p, u_p, z_p, back_p)
    return image_grad.T, text_grad.T, loss.reshape(rows // groups)


def solution(mesh):
    in_specs = (P("blk", None), P("blk", None), P(None, "head"), P(None, "head"))
    out_specs = (P("blk", "head"), P("blk", "head"), P(("blk", "head")))
    return jax.shard_map(body, mesh=mesh, in_specs=in_specs, out_specs=out_specs, check_vma=False)
```

```python
import functools

import jax
import jax.numpy as jnp
from jax import lax
from jax.experimental import pallas as pl
from jax.experimental.pallas import tpu as pltpu
from jax.sharding import PartitionSpec as P

LOGIT_SCALE = 10.0
LOGIT_BIAS = -2.0
EPSILON = 1e-06
PACK = 20_000_000_000
AXES = ("blk", "head")
LANES = 128


class Grid:
    def __init__(self, n_blk, n_head):
        self.n_blk, self.n_head = n_blk, n_head
        self.half = n_blk // 2
        self.depth = 2 * n_head

    def route(self, source):
        return [(source(d), d) for d in range(self.n_blk * self.n_head)]

    def along_blk(self, even, odd):
        def source(d):
            blk, head = divmod(d, self.n_head)
            step = odd if blk % 2 else even
            return (blk + step) % self.n_blk * self.n_head + head

        return self.route(source)

    def along_z(self, even, odd):
        def source(d):
            blk, head = divmod(d, self.n_head)
            z = 2 * head + blk // self.half
            z = (z + (odd if z % 2 else even)) % self.depth
            return (blk % self.half + self.half * (z % 2)) * self.n_head + z // 2

        return self.route(source)


def dot(left, right, left_dim=1, right_dim=0):
    return lax.dot_general(
        left, right, (((left_dim,), (right_dim,)), ((), ())), preferred_element_type=jnp.float32
    )


def project(feats, whole):
    z = dot(feats, whole[...], 1, 1)
    back = 1.0 / jnp.sqrt(jnp.sum(z * z, axis=1, keepdims=True) + EPSILON)
    return z, back, (z * back).astype(jnp.bfloat16)


def window(group, width):
    start = group * width // LANES * LANES
    return pl.multiple_of(start, LANES), pl.multiple_of(group * width - start, 64)


def pack_kernel(skipped, *refs):
    *blocks, out = refs[skipped:]
    at = 0
    for block in blocks:
        out[at : at + block.shape[0], :] = block[...]
        at += block.shape[0]


def primary_kernel(whole, own_r1_r2, r3, u_out, z_out, back_out):
    rows = r3.shape[0]
    for k in range(4):
        block = r3[...] if k == 3 else own_r1_r2[k * rows : (k + 1) * rows, :]
        z, back, u = project(block, whole)
        u_out[k * rows : (k + 1) * rows, :] = u
        if k == 0:
            z_out[...] = z
            back_out[...] = back


def side(u_own, u_others, z, back, cut, logits_ref, at):
    rows = u_own.shape[0]
    logits = LOGIT_SCALE * dot(u_own, u_others[...], 1, 1) + LOGIT_BIAS
    logits_ref[at] = logits
    own = logits[:, :rows]
    turn = jnp.where(
        lax.broadcasted_iota(jnp.int32, own.shape, 0) == lax.broadcasted_iota(jnp.int32, own.shape, 1),
        -1.0,
        1.0,
    )
    w_own = (turn * LOGIT_SCALE / (1.0 + jnp.exp(-turn * own))).astype(jnp.bfloat16)
    w = (LOGIT_SCALE / (1.0 + jnp.exp(-logits[:, rows:]))).astype(jnp.bfloat16)
    g = dot(w_own, u_others[:rows, :]) + dot(w, u_others[rows:, :])
    inner = jnp.sum(g * z, axis=1, keepdims=True)
    dz = (g * back - z * (inner * back * back * back)).astype(jnp.bfloat16)
    return jnp.transpose(dot(dz, cut))


def main_kernel(
    place, whole_q, own, others, whole_p, u_p, z_p, back_p, image_out, text_out, loss_out,
    u_q, logits_ref, grads,
):
    group, swapped = place[0], place[1]
    rows, width = image_out.shape[1], image_out.shape[0]
    start, offset = window(group, width)
    columns = pl.ds(start, grads.shape[1])
    z_q, back_q, u = project(own[...], whole_q)
    u_q[:rows, :] = u
    for k in range(3):
        _, _, u = project(others[k * rows : (k + 1) * rows, :], whole_q)
        u_q[(k + 1) * rows : (k + 2) * rows, :] = u
    grads[0] = side(u_p[:rows, :], u_q, z_p[...], back_p[...], whole_p[:, columns], logits_ref, 0)
    grads[1] = side(u_q[:rows, :], u_p, z_q, back_q, whole_q[:, columns], logits_ref, 1)
    image_out[...] = grads[swapped, pl.ds(offset, width), :].astype(image_out.dtype)
    text_out[...] = grads[1 - swapped, pl.ds(offset, width), :].astype(text_out.dtype)
    quarter = loss_out.shape[1]
    first = pl.multiple_of(group * quarter, 8)
    x = logits_ref[swapped, pl.ds(first, quarter), :]
    on = first + lax.broadcasted_iota(jnp.int32, x.shape, 0) == lax.broadcasted_iota(
        jnp.int32, x.shape, 1
    )
    x = jnp.where(on, -x, x)
    loss = jnp.sum(jnp.maximum(x, 0.0) + jnp.log1p(jnp.exp(-jnp.abs(x))), axis=1, keepdims=True)
    loss_out[...] = jnp.transpose(jnp.broadcast_to(loss, (quarter, LANES)))[:1, :]


ANY = pl.BlockSpec(memory_space=pl.ANY)
VMEM = pl.BlockSpec(memory_space=pltpu.VMEM)
SMEM = pl.BlockSpec(memory_space=pltpu.SMEM)
PARAMS = pltpu.CompilerParams(vmem_limit_bytes=16 * 1024 * 1024)


def cost(flops):
    return pl.CostEstimate(flops=flops, bytes_accessed=1_000_000, transcendentals=0)


def pack(*blocks, after=()):
    rows = sum(block.shape[0] for block in blocks)
    return pl.pallas_call(
        functools.partial(pack_kernel, len(after)),
        out_shape=jax.ShapeDtypeStruct((rows, blocks[0].shape[1]), blocks[0].dtype),
        in_specs=[ANY] * len(after) + [VMEM] * len(blocks),
        out_specs=VMEM,
        compiler_params=PARAMS,
        cost_estimate=cost(PACK),
    )(*after, *blocks)


def body(image_feats, text_feats, image_head, text_head):
    rows, depth = image_feats.shape
    groups = lax.axis_size("head")
    grid = Grid(lax.axis_size("blk"), groups)
    width = image_head.shape[1]
    features = width * groups
    place = jnp.stack([lax.axis_index("head"), lax.axis_index("blk") % 2]).astype(jnp.int32)

    def permute(block, route):
        return lax.ppermute(block, AXES, route)

    even = place[1] == 0
    image_head, text_head = image_head.T, text_head.T
    own_p = jnp.where(even, image_feats, text_feats)
    own_q = jnp.where(even, text_feats, image_feats)
    head_p = jnp.where(even, image_head, text_head)

    swap = grid.along_blk(1, -1)
    near = grid.along_z(-1, 1)
    two_on = grid.along_blk(-2, 2)
    w2 = permute(head_p, grid.along_z(2, -2))
    w1 = permute(head_p, near)
    r1 = permute(own_q, grid.along_blk(-1, 1))
    r2 = permute(own_p, two_on)
    w2 = pack(w2)
    w3 = permute(w2, near)
    r1 = pack(r1, after=(w2,))
    r3 = permute(r1, two_on)
    own_r1_r2 = pack(own_p, r1, r2)
    others = permute(own_r1_r2, swap)
    whole_p = pack(head_p, w1, w2, w3)
    whole_q = permute(whole_p, swap)

    u_p, z_p, back_p = pl.pallas_call(
        primary_kernel,
        out_shape=(
            jax.ShapeDtypeStruct((4 * rows, features), jnp.bfloat16),
            jax.ShapeDtypeStruct((rows, features), jnp.float32),
            jax.ShapeDtypeStruct((rows, 1), jnp.float32),
        ),
        in_specs=[VMEM] * 3,
        out_specs=(VMEM,) * 3,
        compiler_params=PARAMS,
        cost_estimate=cost(80 * rows * depth * features),
    )(whole_p, own_r1_r2, r3)
    image_grad, text_grad, loss = pl.pallas_call(
        main_kernel,
        out_shape=(
            jax.ShapeDtypeStruct((width, rows), jnp.bfloat16),
            jax.ShapeDtypeStruct((width, rows), jnp.bfloat16),
            jax.ShapeDtypeStruct((1, rows // groups), jnp.float32),
        ),
        in_specs=[SMEM] + [VMEM] * 7,
        out_specs=(VMEM,) * 3,
        scratch_shapes=[
            pltpu.VMEM((4 * rows, features), jnp.bfloat16),
            pltpu.VMEM((2, rows, 4 * rows), jnp.float32),
            pltpu.VMEM((2, 2 * LANES, rows), jnp.float32),
        ],
        compiler_params=PARAMS,
        cost_estimate=cost(24 * rows * depth * features),
    )(place, whole_q, own_q, others, whole_p, u_p, z_p, back_p)
    return image_grad.T, text_grad.T, loss.reshape(rows // groups)


def solution(mesh):
    in_specs = (P("blk", None), P("blk", None), P(None, "head"), P(None, "head"))
    out_specs = (P("blk", "head"), P("blk", "head"), P(("blk", "head")))
    return jax.shard_map(body, mesh=mesh, in_specs=in_specs, out_specs=out_specs, check_vma=False)
```

```python
import functools

import jax
import jax.numpy as jnp
from jax import lax
from jax.experimental import pallas as pl
from jax.experimental.pallas import tpu as pltpu
from jax.sharding import PartitionSpec as P

LOGIT_SCALE = 10.0
LOGIT_BIAS = -2.0
EPSILON = 1e-06
PACK = 20_000_000_000
AXES = ("blk", "head")
LANES = 128


class Grid:
    def __init__(self, n_blk, n_head):
        self.n_blk, self.n_head = n_blk, n_head
        self.half = n_blk // 2
        self.depth = 2 * n_head

    def route(self, source):
        return [(source(d), d) for d in range(self.n_blk * self.n_head)]

    def along_blk(self, even, odd):
        def source(d):
            blk, head = divmod(d, self.n_head)
            step = odd if blk % 2 else even
            return (blk + step) % self.n_blk * self.n_head + head

        return self.route(source)

    def along_z(self, even, odd):
        def source(d):
            blk, head = divmod(d, self.n_head)
            z = 2 * head + blk // self.half
            z = (z + (odd if z % 2 else even)) % self.depth
            return (blk % self.half + self.half * (z % 2)) * self.n_head + z // 2

        return self.route(source)


def dot(left, right, left_dim=1, right_dim=0):
    return lax.dot_general(
        left, right, (((left_dim,), (right_dim,)), ((), ())), preferred_element_type=jnp.float32
    )


def project(feats, whole):
    z = dot(feats, whole[...], 1, 1)
    back = 1.0 / jnp.sqrt(jnp.sum(z * z, axis=1, keepdims=True) + EPSILON)
    return z, back, (z * back).astype(jnp.bfloat16)


def window(group, width):
    start = group * width // LANES * LANES
    return pl.multiple_of(start, LANES), pl.multiple_of(group * width - start, 64)


def pack_kernel(skipped, *refs):
    *blocks, out = refs[skipped:]
    at = 0
    for block in blocks:
        out[at : at + block.shape[0], :] = block[...]
        at += block.shape[0]


def primary_kernel(whole, own_r1_r2, r3, u_out, z_out, back_out):
    rows = r3.shape[0]
    for k in range(4):
        block = r3[...] if k == 3 else own_r1_r2[k * rows : (k + 1) * rows, :]
        z, back, u = project(block, whole)
        u_out[k * rows : (k + 1) * rows, :] = u
        if k == 0:
            z_out[...] = z
            back_out[...] = back


def side(u_own, u_others, z, back, cut, logits_ref, at):
    rows = u_own.shape[0]
    logits = LOGIT_SCALE * dot(u_own, u_others[...], 1, 1) + LOGIT_BIAS
    logits_ref[at] = logits
    own = logits[:, :rows]
    turn = jnp.where(
        lax.broadcasted_iota(jnp.int32, own.shape, 0) == lax.broadcasted_iota(jnp.int32, own.shape, 1),
        -1.0,
        1.0,
    )
    w_own = (turn * LOGIT_SCALE / (1.0 + jnp.exp(-turn * own))).astype(jnp.bfloat16)
    w = (LOGIT_SCALE / (1.0 + jnp.exp(-logits[:, rows:]))).astype(jnp.bfloat16)
    g = dot(w_own, u_others[:rows, :]) + dot(w, u_others[rows:, :])
    inner = jnp.sum(g * z, axis=1, keepdims=True)
    dz = (g * back - z * (inner * back * back * back)).astype(jnp.bfloat16)
    return jnp.transpose(dot(dz, cut))


def main_kernel(
    place, whole_q, own, others, whole_p, u_p, z_p, back_p, image_out, text_out, loss_out,
    u_q, logits_ref, grads,
):
    group, swapped = place[0], place[1]
    rows, width = image_out.shape[1], image_out.shape[0]
    start, offset = window(group, width)
    columns = pl.ds(start, grads.shape[1])
    z_q, back_q, u = project(own[...], whole_q)
    u_q[:rows, :] = u
    for k in range(3):
        _, _, u = project(others[k * rows : (k + 1) * rows, :], whole_q)
        u_q[(k + 1) * rows : (k + 2) * rows, :] = u
    grads[0] = side(u_p[:rows, :], u_q, z_p[...], back_p[...], whole_p[:, columns], logits_ref, 0)
    grads[1] = side(u_q[:rows, :], u_p, z_q, back_q, whole_q[:, columns], logits_ref, 1)
    image_out[...] = grads[swapped, pl.ds(offset, width), :].astype(image_out.dtype)
    text_out[...] = grads[1 - swapped, pl.ds(offset, width), :].astype(text_out.dtype)
    quarter = loss_out.shape[1]
    first = pl.multiple_of(group * quarter, 8)
    x = logits_ref[swapped, pl.ds(first, quarter), :]
    on = first + lax.broadcasted_iota(jnp.int32, x.shape, 0) == lax.broadcasted_iota(
        jnp.int32, x.shape, 1
    )
    x = jnp.where(on, -x, x)
    loss = jnp.sum(jnp.maximum(x, 0.0) + jnp.log1p(jnp.exp(-jnp.abs(x))), axis=1, keepdims=True)
    loss_out[...] = jnp.transpose(jnp.broadcast_to(loss, (quarter, LANES)))[:1, :]


ANY = pl.BlockSpec(memory_space=pl.ANY)
VMEM = pl.BlockSpec(memory_space=pltpu.VMEM)
SMEM = pl.BlockSpec(memory_space=pltpu.SMEM)
PARAMS = pltpu.CompilerParams(vmem_limit_bytes=16 * 1024 * 1024)


def cost(flops):
    return pl.CostEstimate(flops=flops, bytes_accessed=1_000_000, transcendentals=0)


def pack(*blocks, after=()):
    rows = sum(block.shape[0] for block in blocks)
    return pl.pallas_call(
        functools.partial(pack_kernel, len(after)),
        out_shape=jax.ShapeDtypeStruct((rows, blocks[0].shape[1]), blocks[0].dtype),
        in_specs=[ANY] * len(after) + [VMEM] * len(blocks),
        out_specs=VMEM,
        compiler_params=PARAMS,
        cost_estimate=cost(PACK),
    )(*after, *blocks)


def body(image_feats, text_feats, image_head, text_head):
    rows, depth = image_feats.shape
    groups = lax.axis_size("head")
    grid = Grid(lax.axis_size("blk"), groups)
    width = image_head.shape[1]
    features = width * groups
    place = jnp.stack([lax.axis_index("head"), lax.axis_index("blk") % 2]).astype(jnp.int32)

    def permute(block, route):
        return lax.ppermute(block, AXES, route)

    even = place[1] == 0
    image_head, text_head = image_head.T, text_head.T
    own_p = jnp.where(even, image_feats, text_feats)
    own_q = jnp.where(even, text_feats, image_feats)
    head_p = jnp.where(even, image_head, text_head)

    swap = grid.along_blk(1, -1)
    near = grid.along_z(-1, 1)
    two_on = grid.along_blk(-2, 2)
    r1 = permute(own_q, grid.along_blk(-1, 1))
    w2 = permute(head_p, grid.along_z(2, -2))
    w1 = permute(head_p, near)
    r2 = permute(own_p, two_on)
    w2 = pack(w2, after=(r1,))
    w3 = permute(w2, near)
    r1 = pack(r1, after=(w2,))
    r3 = permute(r1, two_on)
    own_r1_r2 = pack(own_p, r1, r2)
    others = permute(own_r1_r2, swap)
    whole_p = pack(head_p, w1, w2, w3)
    whole_q = permute(whole_p, swap)

    u_p, z_p, back_p = pl.pallas_call(
        primary_kernel,
        out_shape=(
            jax.ShapeDtypeStruct((4 * rows, features), jnp.bfloat16),
            jax.ShapeDtypeStruct((rows, features), jnp.float32),
            jax.ShapeDtypeStruct((rows, 1), jnp.float32),
        ),
        in_specs=[VMEM] * 3,
        out_specs=(VMEM,) * 3,
        compiler_params=PARAMS,
        cost_estimate=cost(80 * rows * depth * features),
    )(whole_p, own_r1_r2, r3)
    image_grad, text_grad, loss = pl.pallas_call(
        main_kernel,
        out_shape=(
            jax.ShapeDtypeStruct((width, rows), jnp.bfloat16),
            jax.ShapeDtypeStruct((width, rows), jnp.bfloat16),
            jax.ShapeDtypeStruct((1, rows // groups), jnp.float32),
        ),
        in_specs=[SMEM] + [VMEM] * 7,
        out_specs=(VMEM,) * 3,
        scratch_shapes=[
            pltpu.VMEM((4 * rows, features), jnp.bfloat16),
            pltpu.VMEM((2, rows, 4 * rows), jnp.float32),
            pltpu.VMEM((2, 2 * LANES, rows), jnp.float32),
        ],
        compiler_params=PARAMS,
        cost_estimate=cost(24 * rows * depth * features),
    )(place, whole_q, own_q, others, whole_p, u_p, z_p, back_p)
    return image_grad.T, text_grad.T, loss.reshape(rows // groups)


def solution(mesh):
    in_specs = (P("blk", None), P("blk", None), P(None, "head"), P(None, "head"))
    out_specs = (P("blk", "head"), P("blk", "head"), P(("blk", "head")))
    return jax.shard_map(body, mesh=mesh, in_specs=in_specs, out_specs=out_specs, check_vma=False)
```

```python
import functools

import jax
import jax.numpy as jnp
from jax import lax
from jax.experimental import pallas as pl
from jax.experimental.pallas import tpu as pltpu
from jax.sharding import PartitionSpec as P

LOGIT_SCALE = 10.0
LOGIT_BIAS = -2.0
EPSILON = 1e-06
PACK = 20_000_000_000
AXES = ("blk", "head")
LANES = 128


class Grid:
    def __init__(self, n_blk, n_head):
        self.n_blk, self.n_head = n_blk, n_head
        self.half = n_blk // 2
        self.depth = 2 * n_head

    def route(self, source, heads=None):
        heads = heads or range(self.n_head)
        return [(source(d), d) for d in range(self.n_blk * self.n_head) if d % self.n_head in heads]

    def along_blk(self, even, odd, heads=None):
        def source(d):
            blk, head = divmod(d, self.n_head)
            step = odd if blk % 2 else even
            return (blk + step) % self.n_blk * self.n_head + head

        return self.route(source, heads)

    def along_z(self, even, odd):
        def source(d):
            blk, head = divmod(d, self.n_head)
            z = 2 * head + blk // self.half
            z = (z + (odd if z % 2 else even)) % self.depth
            return (blk % self.half + self.half * (z % 2)) * self.n_head + z // 2

        return self.route(source)


def dot(left, right, left_dim=1, right_dim=0):
    return lax.dot_general(
        left, right, (((left_dim,), (right_dim,)), ((), ())), preferred_element_type=jnp.float32
    )


def project(feats, whole):
    z = dot(feats, whole[...], 1, 1)
    back = 1.0 / jnp.sqrt(jnp.sum(z * z, axis=1, keepdims=True) + EPSILON)
    return z, back, (z * back).astype(jnp.bfloat16)


def window(group, width):
    start = group * width // LANES * LANES
    return pl.multiple_of(start, LANES), pl.multiple_of(group * width - start, 64)


def pack_kernel(skipped, *refs):
    *blocks, out = refs[skipped:]
    at = 0
    for block in blocks:
        out[at : at + block.shape[0], :] = block[...]
        at += block.shape[0]


def either_kernel(place, early, late, _, out):
    @pl.when(place[2] != 0)
    def _():
        out[...] = early[...]

    @pl.when(place[2] == 0)
    def _():
        out[...] = late[...]


def project_all(blocks, whole, u_out, z_out, back_out):
    rows = z_out.shape[0]
    for k, block in enumerate(blocks):
        z, back, u = project(block, whole)
        u_out[k * rows : (k + 1) * rows, :] = u
        if k == 0:
            z_out[...] = z
            back_out[...] = back


def primary_kernel(whole, blocks, u_out, z_out, back_out):
    rows = z_out.shape[0]
    project_all([blocks[k * rows : (k + 1) * rows, :] for k in range(3)], whole, u_out, z_out, back_out)


def weights_of(logits, turned):
    if turned:
        on = lax.broadcasted_iota(jnp.int32, logits.shape, 0) == lax.broadcasted_iota(
            jnp.int32, logits.shape, 1
        )
        turn = jnp.where(on, -1.0, 1.0)
        return (turn * LOGIT_SCALE / (1.0 + jnp.exp(-turn * logits))).astype(jnp.bfloat16)
    return (LOGIT_SCALE / (1.0 + jnp.exp(-logits))).astype(jnp.bfloat16)


def side(place, u_own, met, z, back, whole, logits_ref, grad_ref, grad_out, loss_out):
    group, width = place[0], grad_out.shape[0]
    rows = u_own.shape[0]
    at, g = 0, None
    for u in met:
        logits = LOGIT_SCALE * dot(u_own, u, 1, 1) + LOGIT_BIAS
        logits_ref[:, at : at + u.shape[0]] = logits
        if at == 0:
            g = dot(weights_of(logits[:, :rows], True), u[:rows, :])
            if u.shape[0] > rows:
                g = g + dot(weights_of(logits[:, rows:], False), u[rows:, :])
        else:
            g = g + dot(weights_of(logits, False), u)
        at += u.shape[0]
    inner = jnp.sum(g * z, axis=1, keepdims=True)
    dz = (g * back - z * (inner * back * back * back)).astype(jnp.bfloat16)
    start, offset = window(group, width)
    grad_ref[...] = jnp.transpose(dot(dz, whole[:, pl.ds(start, grad_ref.shape[0])]))
    grad_out[...] = grad_ref[pl.ds(offset, width), :].astype(grad_out.dtype)
    quarter = loss_out.shape[1]
    first = pl.multiple_of(group * quarter, 8)
    x = logits_ref[pl.ds(first, quarter), :]
    on = first + lax.broadcasted_iota(jnp.int32, x.shape, 0) == lax.broadcasted_iota(
        jnp.int32, x.shape, 1
    )
    x = jnp.where(on, -x, x)
    loss = jnp.sum(jnp.maximum(x, 0.0) + jnp.log1p(jnp.exp(-jnp.abs(x))), axis=1, keepdims=True)
    loss_out[...] = jnp.transpose(jnp.broadcast_to(loss, (quarter, LANES)))[:1, :]


def primary_side_kernel(
    place, whole_q, own_q, others, whole_p, u_p, z_p, back_p,
    grad_out, loss_out, u_out, z_out, back_out, u_q, logits_ref, grad_ref,
):
    rows = own_q.shape[0]
    blocks = [own_q[...]] + [others[k * rows : (k + 1) * rows, :] for k in range(3)]
    project_all(blocks, whole_q, u_q, z_out, back_out)
    u_out[...] = u_q[:rows, :]
    side(
        place, u_p[:rows, :], [u_q[...]], z_p[...], back_p[...], whole_p, logits_ref, grad_ref,
        grad_out, loss_out,
    )


def secondary_side_kernel(
    place, whole_p, r3, u_p, whole_q, u_q, z_q, back_q, grad_p, loss_p,
    image_out, text_out, loss_out, logits_ref, grad_ref, grad_q,
):
    _, _, u_3 = project(r3[...], whole_p)
    side(
        place, u_q[...], [u_p[...], u_3], z_q[...], back_q[...], whole_q, logits_ref, grad_ref,
        grad_q, loss_out,
    )

    @pl.when(place[1] == 0)
    def _():
        image_out[...] = grad_p[...]
        text_out[...] = grad_q[...]
        loss_out[...] = loss_p[...]

    @pl.when(place[1] != 0)
    def _():
        image_out[...] = grad_q[...]
        text_out[...] = grad_p[...]


ANY = pl.BlockSpec(memory_space=pl.ANY)
VMEM = pl.BlockSpec(memory_space=pltpu.VMEM)
SMEM = pl.BlockSpec(memory_space=pltpu.SMEM)
PARAMS = pltpu.CompilerParams(vmem_limit_bytes=16 * 1024 * 1024)


def cost(flops):
    return pl.CostEstimate(flops=flops, bytes_accessed=1_000_000, transcendentals=0)


def pack(*blocks, after=()):
    rows = sum(block.shape[0] for block in blocks)
    return pl.pallas_call(
        functools.partial(pack_kernel, len(after)),
        out_shape=jax.ShapeDtypeStruct((rows, blocks[0].shape[1]), blocks[0].dtype),
        in_specs=[ANY] * len(after) + [VMEM] * len(blocks),
        out_specs=VMEM,
        compiler_params=PARAMS,
        cost_estimate=cost(PACK),
    )(*after, *blocks)


def body(image_feats, text_feats, image_head, text_head):
    rows, depth = image_feats.shape
    groups = lax.axis_size("head")
    grid = Grid(lax.axis_size("blk"), groups)
    width = image_head.shape[1]
    features = width * groups
    group = lax.axis_index("head")
    place = jnp.stack([group, lax.axis_index("blk") % 2, group < groups // 2]).astype(jnp.int32)

    def permute(block, route):
        return lax.ppermute(block, AXES, route)

    even = place[1] == 0
    image_head, text_head = image_head.T, text_head.T
    own_p = jnp.where(even, image_feats, text_feats)
    own_q = jnp.where(even, text_feats, image_feats)
    head_p = jnp.where(even, image_head, text_head)

    swap = grid.along_blk(1, -1)
    near = grid.along_z(-1, 1)
    two_on = grid.along_blk(-2, 2)
    early, late = range(groups // 2), range(groups // 2, groups)
    early_1 = permute(own_q, grid.along_blk(-1, 1, early))
    w2 = permute(head_p, grid.along_z(2, -2))
    w1 = permute(head_p, near)
    late_1 = permute(own_q, grid.along_blk(-1, 1, late))
    r2 = permute(own_p, two_on)
    w2 = pack(w2, after=(early_1,))
    w3 = permute(w2, near)
    r1 = pl.pallas_call(
        either_kernel,
        out_shape=jax.ShapeDtypeStruct((rows, depth), own_q.dtype),
        in_specs=[SMEM, VMEM, VMEM, ANY],
        out_specs=VMEM,
        compiler_params=PARAMS,
        cost_estimate=cost(PACK),
    )(place, early_1, late_1, w2)
    r3 = permute(r1, two_on)
    own_r1_r2 = pack(own_p, r1, r2)
    others = permute(own_r1_r2, swap)
    whole_p = pack(head_p, w1, w2, w3)
    whole_q = permute(whole_p, swap)

    own_z = jax.ShapeDtypeStruct((rows, features), jnp.float32)
    own_back = jax.ShapeDtypeStruct((rows, 1), jnp.float32)
    grad = jax.ShapeDtypeStruct((width, rows), jnp.bfloat16)
    loss = jax.ShapeDtypeStruct((1, rows // groups), jnp.float32)
    scratch = [
        pltpu.VMEM((rows, 4 * rows), jnp.float32),
        pltpu.VMEM((2 * LANES, rows), jnp.float32),
    ]
    u_p, z_p, back_p = pl.pallas_call(
        primary_kernel,
        out_shape=(jax.ShapeDtypeStruct((3 * rows, features), jnp.bfloat16), own_z, own_back),
        in_specs=[VMEM] * 2,
        out_specs=(VMEM,) * 3,
        compiler_params=PARAMS,
        cost_estimate=cost(80 * rows * depth * features),
    )(whole_p, own_r1_r2)
    grad_p, loss_p, u_q, z_q, back_q = pl.pallas_call(
        primary_side_kernel,
        out_shape=(
            grad, loss, jax.ShapeDtypeStruct((rows, features), jnp.bfloat16), own_z, own_back,
        ),
        in_specs=[SMEM] + [VMEM] * 7,
        out_specs=(VMEM,) * 5,
        scratch_shapes=[pltpu.VMEM((4 * rows, features), jnp.bfloat16)] + scratch,
        compiler_params=PARAMS,
        cost_estimate=cost(24 * rows * depth * features),
    )(place, whole_q, own_q, others, whole_p, u_p, z_p, back_p)
    image_grad, text_grad, loss = pl.pallas_call(
        secondary_side_kernel,
        out_shape=(grad, grad, loss),
        in_specs=[SMEM] + [VMEM] * 9,
        out_specs=(VMEM,) * 3,
        scratch_shapes=scratch + [pltpu.VMEM(grad.shape, grad.dtype)],
        compiler_params=PARAMS,
        cost_estimate=cost(12 * rows * depth * features),
    )(place, whole_p, r3, u_p, whole_q, u_q, z_q, back_q, grad_p, loss_p)
    return image_grad.T, text_grad.T, loss.reshape(rows // groups)


def solution(mesh):
    in_specs = (P("blk", None), P("blk", None), P(None, "head"), P(None, "head"))
    out_specs = (P("blk", "head"), P("blk", "head"), P(("blk", "head")))
    return jax.shard_map(body, mesh=mesh, in_specs=in_specs, out_specs=out_specs, check_vma=False)
```

```python
import functools

import jax
import jax.numpy as jnp
from jax import lax
from jax.experimental import pallas as pl
from jax.experimental.pallas import tpu as pltpu
from jax.sharding import PartitionSpec as P

LOGIT_SCALE = 10.0
LOGIT_BIAS = -2.0
EPSILON = 1e-06
PACK = 20_000_000_000
AXES = ("blk", "head")
LANES = 128


class Grid:
    def __init__(self, n_blk, n_head):
        self.n_blk, self.n_head = n_blk, n_head
        self.half = n_blk // 2
        self.depth = 2 * n_head

    def route(self, source, heads=None):
        heads = heads or range(self.n_head)
        return [(source(d), d) for d in range(self.n_blk * self.n_head) if d % self.n_head in heads]

    def along_blk(self, even, odd, heads=None):
        def source(d):
            blk, head = divmod(d, self.n_head)
            step = odd if blk % 2 else even
            return (blk + step) % self.n_blk * self.n_head + head

        return self.route(source, heads)

    def along_z(self, even, odd):
        def source(d):
            blk, head = divmod(d, self.n_head)
            z = 2 * head + blk // self.half
            z = (z + (odd if z % 2 else even)) % self.depth
            return (blk % self.half + self.half * (z % 2)) * self.n_head + z // 2

        return self.route(source)


def dot(left, right, left_dim=1, right_dim=0):
    return lax.dot_general(
        left, right, (((left_dim,), (right_dim,)), ((), ())), preferred_element_type=jnp.float32
    )


def project(feats, whole):
    z = dot(feats, whole[...], 1, 1)
    back = 1.0 / jnp.sqrt(jnp.sum(z * z, axis=1, keepdims=True) + EPSILON)
    return z, back, (z * back).astype(jnp.bfloat16)


def window(group, width):
    start = group * width // LANES * LANES
    return pl.multiple_of(start, LANES), pl.multiple_of(group * width - start, 64)


def pack_kernel(skipped, *refs):
    *blocks, out = refs[skipped:]
    at = 0
    for block in blocks:
        out[at : at + block.shape[0], :] = block[...]
        at += block.shape[0]


def either_kernel(place, early, late, _, out):
    @pl.when(place[2] != 0)
    def _():
        out[...] = early[...]

    @pl.when(place[2] == 0)
    def _():
        out[...] = late[...]


def project_all(blocks, whole, u_out, z_out, back_out):
    rows = z_out.shape[0]
    for k, block in enumerate(blocks):
        z, back, u = project(block, whole)
        u_out[k * rows : (k + 1) * rows, :] = u
        if k == 0:
            z_out[...] = z
            back_out[...] = back


def primary_kernel(whole, blocks, u_out, z_out, back_out):
    rows = z_out.shape[0]
    project_all([blocks[k * rows : (k + 1) * rows, :] for k in range(3)], whole, u_out, z_out, back_out)


def side(u_own, u_others, z, back, cut, logits_ref, at):
    rows = u_own.shape[0]
    logits = LOGIT_SCALE * dot(u_own, u_others[...], 1, 1) + LOGIT_BIAS
    logits_ref[at] = logits
    own = logits[:, :rows]
    turn = jnp.where(
        lax.broadcasted_iota(jnp.int32, own.shape, 0) == lax.broadcasted_iota(jnp.int32, own.shape, 1),
        -1.0,
        1.0,
    )
    w_own = (turn * LOGIT_SCALE / (1.0 + jnp.exp(-turn * own))).astype(jnp.bfloat16)
    w = (LOGIT_SCALE / (1.0 + jnp.exp(-logits[:, rows:]))).astype(jnp.bfloat16)
    g = dot(w_own, u_others[:rows, :]) + dot(w, u_others[rows:, :])
    inner = jnp.sum(g * z, axis=1, keepdims=True)
    dz = (g * back - z * (inner * back * back * back)).astype(jnp.bfloat16)
    return jnp.transpose(dot(dz, cut))


def secondary_kernel(whole, own, others, u_out, z_out, back_out):
    rows = z_out.shape[0]
    blocks = [own[...]] + [others[k * rows : (k + 1) * rows, :] for k in range(3)]
    project_all(blocks, whole, u_out, z_out, back_out)


def sides_kernel(
    place, whole_p, r3, u_p3, z_p, back_p, whole_q, u_q, z_q, back_q, image_out, text_out, loss_out,
    u_p, logits_ref, grads,
):
    group, swapped = place[0], place[1]
    rows, width = image_out.shape[1], image_out.shape[0]
    start, offset = window(group, width)
    columns = pl.ds(start, grads.shape[1])
    _, _, u = project(r3[...], whole_p)
    u_p[3 * rows :, :] = u
    u_p[: 3 * rows, :] = u_p3[...]
    grads[0] = side(u_p[:rows, :], u_q, z_p[...], back_p[...], whole_p[:, columns], logits_ref, 0)
    grads[1] = side(u_q[:rows, :], u_p, z_q[...], back_q[...], whole_q[:, columns], logits_ref, 1)
    image_out[...] = grads[swapped, pl.ds(offset, width), :].astype(image_out.dtype)
    text_out[...] = grads[1 - swapped, pl.ds(offset, width), :].astype(text_out.dtype)
    quarter = loss_out.shape[1]
    first = pl.multiple_of(group * quarter, 8)
    x = logits_ref[swapped, pl.ds(first, quarter), :]
    on = first + lax.broadcasted_iota(jnp.int32, x.shape, 0) == lax.broadcasted_iota(
        jnp.int32, x.shape, 1
    )
    x = jnp.where(on, -x, x)
    loss = jnp.sum(jnp.maximum(x, 0.0) + jnp.log1p(jnp.exp(-jnp.abs(x))), axis=1, keepdims=True)
    loss_out[...] = jnp.transpose(jnp.broadcast_to(loss, (quarter, LANES)))[:1, :]


ANY = pl.BlockSpec(memory_space=pl.ANY)
VMEM = pl.BlockSpec(memory_space=pltpu.VMEM)
SMEM = pl.BlockSpec(memory_space=pltpu.SMEM)
PARAMS = pltpu.CompilerParams(vmem_limit_bytes=16 * 1024 * 1024)


def cost(flops):
    return pl.CostEstimate(flops=flops, bytes_accessed=1_000_000, transcendentals=0)


def pack(*blocks, after=()):
    rows = sum(block.shape[0] for block in blocks)
    return pl.pallas_call(
        functools.partial(pack_kernel, len(after)),
        out_shape=jax.ShapeDtypeStruct((rows, blocks[0].shape[1]), blocks[0].dtype),
        in_specs=[ANY] * len(after) + [VMEM] * len(blocks),
        out_specs=VMEM,
        compiler_params=PARAMS,
        cost_estimate=cost(PACK),
    )(*after, *blocks)


def body(image_feats, text_feats, image_head, text_head):
    rows, depth = image_feats.shape
    groups = lax.axis_size("head")
    grid = Grid(lax.axis_size("blk"), groups)
    width = image_head.shape[1]
    features = width * groups
    group = lax.axis_index("head")
    place = jnp.stack([group, lax.axis_index("blk") % 2, group < groups // 2]).astype(jnp.int32)

    def permute(block, route):
        return lax.ppermute(block, AXES, route)

    even = place[1] == 0
    image_head, text_head = image_head.T, text_head.T
    own_p = jnp.where(even, image_feats, text_feats)
    own_q = jnp.where(even, text_feats, image_feats)
    head_p = jnp.where(even, image_head, text_head)

    swap = grid.along_blk(1, -1)
    near = grid.along_z(-1, 1)
    two_on = grid.along_blk(-2, 2)
    early, late = range(groups // 2), range(groups // 2, groups)
    early_1 = permute(own_q, grid.along_blk(-1, 1, early))
    w2 = permute(head_p, grid.along_z(2, -2))
    w1 = permute(head_p, near)
    late_1 = permute(own_q, grid.along_blk(-1, 1, late))
    r2 = permute(own_p, two_on)
    w2 = pack(w2, after=(early_1,))
    w3 = permute(w2, near)
    r1 = pl.pallas_call(
        either_kernel,
        out_shape=jax.ShapeDtypeStruct((rows, depth), own_q.dtype),
        in_specs=[SMEM, VMEM, VMEM, ANY],
        out_specs=VMEM,
        compiler_params=PARAMS,
        cost_estimate=cost(PACK),
    )(place, early_1, late_1, w2)
    r3 = permute(r1, two_on)
    own_r1_r2 = pack(own_p, r1, r2)
    others = permute(own_r1_r2, swap)
    whole_p = pack(head_p, w1, w2, w3)
    whole_q = permute(whole_p, swap)

    own_z = jax.ShapeDtypeStruct((rows, features), jnp.float32)
    own_back = jax.ShapeDtypeStruct((rows, 1), jnp.float32)
    grad = jax.ShapeDtypeStruct((width, rows), jnp.bfloat16)
    loss = jax.ShapeDtypeStruct((1, rows // groups), jnp.float32)
    u_p, z_p, back_p = pl.pallas_call(
        primary_kernel,
        out_shape=(jax.ShapeDtypeStruct((3 * rows, features), jnp.bfloat16), own_z, own_back),
        in_specs=[VMEM] * 2,
        out_specs=(VMEM,) * 3,
        compiler_params=PARAMS,
        cost_estimate=cost(80 * rows * depth * features),
    )(whole_p, own_r1_r2)
    u_q, z_q, back_q = pl.pallas_call(
        secondary_kernel,
        out_shape=(jax.ShapeDtypeStruct((4 * rows, features), jnp.bfloat16), own_z, own_back),
        in_specs=[VMEM] * 3,
        out_specs=(VMEM,) * 3,
        compiler_params=PARAMS,
        cost_estimate=cost(24 * rows * depth * features),
    )(whole_q, own_q, others)
    image_grad, text_grad, loss = pl.pallas_call(
        sides_kernel,
        out_shape=(grad, grad, loss),
        in_specs=[SMEM] + [VMEM] * 9,
        out_specs=(VMEM,) * 3,
        scratch_shapes=[
            pltpu.VMEM((4 * rows, features), jnp.bfloat16),
            pltpu.VMEM((2, rows, 4 * rows), jnp.float32),
            pltpu.VMEM((2, 2 * LANES, rows), jnp.float32),
        ],
        compiler_params=PARAMS,
        cost_estimate=cost(12 * rows * depth * features),
    )(place, whole_p, r3, u_p, z_p, back_p, whole_q, u_q, z_q, back_q)
    return image_grad.T, text_grad.T, loss.reshape(rows // groups)


def solution(mesh):
    in_specs = (P("blk", None), P("blk", None), P(None, "head"), P(None, "head"))
    out_specs = (P("blk", "head"), P("blk", "head"), P(("blk", "head")))
    return jax.shard_map(body, mesh=mesh, in_specs=in_specs, out_specs=out_specs, check_vma=False)
```

```python
import functools

import jax
import jax.numpy as jnp
from jax import lax
from jax.experimental import pallas as pl
from jax.experimental.pallas import tpu as pltpu
from jax.sharding import PartitionSpec as P

LOGIT_SCALE = 10.0
LOGIT_BIAS = -2.0
EPSILON = 1e-06
PACK = 20_000_000_000
AXES = ("blk", "head")
LANES = 128


class Grid:
    def __init__(self, n_blk, n_head):
        self.n_blk, self.n_head = n_blk, n_head
        self.half = n_blk // 2
        self.depth = 2 * n_head

    def route(self, source, heads=None):
        heads = heads or range(self.n_head)
        return [(source(d), d) for d in range(self.n_blk * self.n_head) if d % self.n_head in heads]

    def along_blk(self, even, odd, heads=None):
        def source(d):
            blk, head = divmod(d, self.n_head)
            step = odd if blk % 2 else even
            return (blk + step) % self.n_blk * self.n_head + head

        return self.route(source, heads)

    def along_z(self, even, odd):
        def source(d):
            blk, head = divmod(d, self.n_head)
            z = 2 * head + blk // self.half
            z = (z + (odd if z % 2 else even)) % self.depth
            return (blk % self.half + self.half * (z % 2)) * self.n_head + z // 2

        return self.route(source)


def dot(left, right, left_dim=1, right_dim=0):
    return lax.dot_general(
        left, right, (((left_dim,), (right_dim,)), ((), ())), preferred_element_type=jnp.float32
    )


def project(feats, whole):
    z = dot(feats, whole[...], 1, 1)
    back = 1.0 / jnp.sqrt(jnp.sum(z * z, axis=1, keepdims=True) + EPSILON)
    return z, back, (z * back).astype(jnp.bfloat16)


def window(group, width):
    start = group * width // LANES * LANES
    return pl.multiple_of(start, LANES), pl.multiple_of(group * width - start, 64)


def pack_kernel(skipped, *refs):
    *blocks, out = refs[skipped:]
    at = 0
    for block in blocks:
        out[at : at + block.shape[0], :] = block[...]
        at += block.shape[0]


def either_kernel(early, late, _, out):
    out[...] = early[...] + late[...]


def project_all(blocks, whole, u_out, z_out, back_out):
    rows = z_out.shape[0]
    for k, block in enumerate(blocks):
        z, back, u = project(block, whole)
        u_out[k * rows : (k + 1) * rows, :] = u
        if k == 0:
            z_out[...] = z
            back_out[...] = back


def primary_kernel(whole, blocks, u_out, z_out, back_out):
    rows = z_out.shape[0]
    project_all([blocks[k * rows : (k + 1) * rows, :] for k in range(3)], whole, u_out, z_out, back_out)


def side(u_own, u_others, z, back, cut, logits_ref, at):
    rows = u_own.shape[0]
    logits = LOGIT_SCALE * dot(u_own, u_others[...], 1, 1) + LOGIT_BIAS
    logits_ref[at] = logits
    own = logits[:, :rows]
    turn = jnp.where(
        lax.broadcasted_iota(jnp.int32, own.shape, 0) == lax.broadcasted_iota(jnp.int32, own.shape, 1),
        -1.0,
        1.0,
    )
    w_own = (turn * LOGIT_SCALE / (1.0 + jnp.exp(-turn * own))).astype(jnp.bfloat16)
    w = (LOGIT_SCALE / (1.0 + jnp.exp(-logits[:, rows:]))).astype(jnp.bfloat16)
    g = dot(w_own, u_others[:rows, :]) + dot(w, u_others[rows:, :])
    inner = jnp.sum(g * z, axis=1, keepdims=True)
    dz = (g * back - z * (inner * back * back * back)).astype(jnp.bfloat16)
    return jnp.transpose(dot(dz, cut))


def secondary_kernel(whole, own, others, u_out, z_out, back_out):
    rows = z_out.shape[0]
    blocks = [own[...]] + [others[k * rows : (k + 1) * rows, :] for k in range(3)]
    project_all(blocks, whole, u_out, z_out, back_out)


def sides_kernel(
    whole_p, r3, u_p3, z_p, back_p, whole_q, u_q, z_q, back_q, image_out, text_out, loss_out,
    u_p, logits_ref, grads,
):
    group, swapped = lax.axis_index("head"), lax.rem(lax.axis_index("blk"), 2)
    rows, width = image_out.shape[1], image_out.shape[0]
    start, offset = window(group, width)
    columns = pl.ds(start, grads.shape[1])
    _, _, u = project(r3[...], whole_p)
    u_p[3 * rows :, :] = u
    u_p[: 3 * rows, :] = u_p3[...]
    grads[0] = side(u_p[:rows, :], u_q, z_p[...], back_p[...], whole_p[:, columns], logits_ref, 0)
    grads[1] = side(u_q[:rows, :], u_p, z_q[...], back_q[...], whole_q[:, columns], logits_ref, 1)
    image_out[...] = grads[swapped, pl.ds(offset, width), :].astype(image_out.dtype)
    text_out[...] = grads[1 - swapped, pl.ds(offset, width), :].astype(text_out.dtype)
    quarter = loss_out.shape[1]
    first = pl.multiple_of(group * quarter, 8)
    x = logits_ref[swapped, pl.ds(first, quarter), :]
    on = first + lax.broadcasted_iota(jnp.int32, x.shape, 0) == lax.broadcasted_iota(
        jnp.int32, x.shape, 1
    )
    x = jnp.where(on, -x, x)
    loss = jnp.sum(jnp.maximum(x, 0.0) + jnp.log1p(jnp.exp(-jnp.abs(x))), axis=1, keepdims=True)
    loss_out[...] = jnp.transpose(jnp.broadcast_to(loss, (quarter, LANES)))[:1, :]


ANY = pl.BlockSpec(memory_space=pl.ANY)
VMEM = pl.BlockSpec(memory_space=pltpu.VMEM)
PARAMS = pltpu.CompilerParams(vmem_limit_bytes=16 * 1024 * 1024)


def cost(flops):
    return pl.CostEstimate(flops=flops, bytes_accessed=1_000_000, transcendentals=0)


def pack(*blocks, after=()):
    rows = sum(block.shape[0] for block in blocks)
    return pl.pallas_call(
        functools.partial(pack_kernel, len(after)),
        out_shape=jax.ShapeDtypeStruct((rows, blocks[0].shape[1]), blocks[0].dtype),
        in_specs=[ANY] * len(after) + [VMEM] * len(blocks),
        out_specs=VMEM,
        compiler_params=PARAMS,
        cost_estimate=cost(PACK),
    )(*after, *blocks)


def body(image_feats, text_feats, image_head, text_head):
    rows, depth = image_feats.shape
    groups = lax.axis_size("head")
    grid = Grid(lax.axis_size("blk"), groups)
    width = image_head.shape[1]
    features = width * groups

    def permute(block, route):
        return lax.ppermute(block, AXES, route)

    even = lax.axis_index("blk") % 2 == 0
    image_head, text_head = image_head.T, text_head.T
    own_p = jnp.where(even, image_feats, text_feats)
    own_q = jnp.where(even, text_feats, image_feats)
    head_p = jnp.where(even, image_head, text_head)

    swap = grid.along_blk(1, -1)
    near = grid.along_z(-1, 1)
    two_on = grid.along_blk(-2, 2)
    early, late = range(groups // 2), range(groups // 2, groups)
    early_1 = permute(own_q, grid.along_blk(-1, 1, early))
    w2 = permute(head_p, grid.along_z(2, -2))
    w1 = permute(head_p, near)
    late_1 = permute(own_q, grid.along_blk(-1, 1, late))
    r2 = permute(own_p, two_on)
    w2 = pack(w2, after=(early_1,))
    w3 = permute(w2, near)
    r1 = pl.pallas_call(
        either_kernel,
        out_shape=jax.ShapeDtypeStruct((rows, depth), own_q.dtype),
        in_specs=[VMEM, VMEM, ANY],
        out_specs=VMEM,
        compiler_params=PARAMS,
        cost_estimate=cost(PACK),
    )(early_1, late_1, w2)
    r3 = permute(r1, two_on)
    own_r1_r2 = pack(own_p, r1, r2)
    others = permute(own_r1_r2, swap)
    whole_p = pack(head_p, w1, w2, w3)
    whole_q = permute(whole_p, swap)

    own_z = jax.ShapeDtypeStruct((rows, features), jnp.float32)
    own_back = jax.ShapeDtypeStruct((rows, 1), jnp.float32)
    grad = jax.ShapeDtypeStruct((width, rows), jnp.bfloat16)
    loss = jax.ShapeDtypeStruct((1, rows // groups), jnp.float32)
    u_p, z_p, back_p = pl.pallas_call(
        primary_kernel,
        out_shape=(jax.ShapeDtypeStruct((3 * rows, features), jnp.bfloat16), own_z, own_back),
        in_specs=[VMEM] * 2,
        out_specs=(VMEM,) * 3,
        compiler_params=PARAMS,
        cost_estimate=cost(80 * rows * depth * features),
    )(whole_p, own_r1_r2)
    u_q, z_q, back_q = pl.pallas_call(
        secondary_kernel,
        out_shape=(jax.ShapeDtypeStruct((4 * rows, features), jnp.bfloat16), own_z, own_back),
        in_specs=[VMEM] * 3,
        out_specs=(VMEM,) * 3,
        compiler_params=PARAMS,
        cost_estimate=cost(24 * rows * depth * features),
    )(whole_q, own_q, others)
    image_grad, text_grad, loss = pl.pallas_call(
        sides_kernel,
        out_shape=(grad, grad, loss),
        in_specs=[VMEM] * 9,
        out_specs=(VMEM,) * 3,
        scratch_shapes=[
            pltpu.VMEM((4 * rows, features), jnp.bfloat16),
            pltpu.VMEM((2, rows, 4 * rows), jnp.float32),
            pltpu.VMEM((2, 2 * LANES, rows), jnp.float32),
        ],
        compiler_params=PARAMS,
        cost_estimate=cost(12 * rows * depth * features),
    )(whole_p, r3, u_p, z_p, back_p, whole_q, u_q, z_q, back_q)
    return image_grad.T, text_grad.T, loss.reshape(rows // groups)


def solution(mesh):
    in_specs = (P("blk", None), P("blk", None), P(None, "head"), P(None, "head"))
    out_specs = (P("blk", "head"), P("blk", "head"), P(("blk", "head")))
    return jax.shard_map(body, mesh=mesh, in_specs=in_specs, out_specs=out_specs, check_vma=False)
```
